32 devices in a mesh: section: 8 (over z, x), sp: 4 (over y, core).
Axes of the slice: x: 2, y: 2, z: 4, core: 2. Of those that a mesh axis runs over, the one named last changes fastest.
Arguments:
- latents: bfloat16 [4, 64, 3072], P(None, 'sp'), may hold values from -6 to 6
- in_flight: bfloat16 [8, 64, 3072], P('section', 'sp'), may hold values from -6 to 6
- modulation: float32 [8, 3, 3072], P('section'), may hold values from -3 to 3
- w_qkv: bfloat16 [8, 3072, 3, 2048], P('section', None, None, 'sp'), may hold values from -0.109375 to 0.109375
- w_expand: bfloat16 [8, 3072, 10240], P('section', None, 'sp'), may hold values from -0.109375 to 0.109375
- qk_gain: float32 [8, 2, 128], P('section'), may hold values from 0.3 to 3
- w_out: bfloat16 [8, 2048, 3072], P('section', 'sp'), may hold values from -0.0546875 to 0.0546875
- w_contract: bfloat16 [8, 10240, 3072], P('section', 'sp'), may hold values from -0.0546875 to 0.0546875
- stale_kv: bfloat16 [8, 2, 256, 2048], P('section', None, None, 'sp'), may hold values from -400 to 400, as said below
Outputs:
- section_out: bfloat16 [8, 4, 64, 3072], P('section', None, 'sp')
- fresh_kv: bfloat16 [8, 4, 2, 64, 2048], P('section', None, None, None, 'sp')
The draws below stay inside these ranges and needn't reach their ends.
Inputs may be any that keep to these rules, and one draw needn't show every extreme that they name: `stale_kv`: entry 0 holds keys and entry 1 values; patch m occupies rows m * 64 to (m + 1) * 64 - 1.
All inputs are finite; a program needn't handle non-finite values.
Results may differ from the reference program's by a relative error of at most 0.03.
Values may be sent and summed in bfloat16 or wider, within the bound.
No kernel may reach another device: no remote copies, remote signals or barrier semaphores. Data moves between devices by JAX's collectives and lax.ppermute only.
A program may use at most 128 MiB of HBM per device.

```python
import math
import jax
import jax.numpy as jnp
from jax import lax

D = 3072
HD = 128
HEADS = 16
FF = 10240
MICRO = 4
SECTIONS = 8
PATCH = 64
CONTEXT = 256
HEADS_DEV = 4
FF_DEV = 2560
N_SP = 4


def draw_stale_kv(key, part):
    key = jax.random.fold_in(key, 7)
    factors = jnp.exp(jax.random.uniform(jax.random.fold_in(key, 1), (SECTIONS, 2, CONTEXT, 1), jnp.float32, math.log(0.3), math.log(2.5)))
    entries = jax.random.normal(jax.random.fold_in(key, 2), (SECTIONS, 2, CONTEXT, HEADS * HD), jnp.float32) * factors
    return entries.astype(jnp.bfloat16)


def levels(key, dims, pieces, smallest, top_value):
    def one(dim, shards_of):
        heights = jax.random.uniform(jax.random.fold_in(jax.random.fold_in(key, 6), dim), (shards_of,), jnp.float32, smallest / len(pieces), top_value / len(pieces))
        return jnp.repeat(jnp.exp(heights), dims[dim] // shards_of).reshape((-1,) + (1,) * (len(dims) - dim - 1))

    level = one(*pieces[0])
    for cut in pieces[1:]:
        level = level * one(*cut)
    return level


def normal_values(stream_key, extent, scale, bound, split=(), kind=jnp.bfloat16):
    array = scale * jax.random.normal(stream_key, extent, jnp.float32)
    if split:
        array = array * levels(stream_key, extent, split, -0.22, 0.18)
    return jnp.clip(array, -bound, bound).astype(kind)


def setup_inputs(seed: int = 0) -> dict:
    keys = jax.random.split(jax.random.key(seed), 10)
    return {
        "latents": normal_values(keys[0], (MICRO, PATCH, D), 1.0, 6.0, ((1, 4),)),
        "in_flight": normal_values(keys[1], (SECTIONS, PATCH, D), 1.0, 6.0, ((0, 8), (1, 4))),
        "modulation": normal_values(keys[2], (SECTIONS, 3, D), 0.5, 3.0, ((0, 8),), jnp.float32),
        "w_qkv": normal_values(keys[3], (SECTIONS, D, 3, HEADS * HD), D ** -0.5, 0.109375, ((0, 8), (3, 4))),
        "w_expand": normal_values(keys[4], (SECTIONS, D, FF), D ** -0.5, 0.109375, ((0, 8), (2, 4))),
        "qk_gain": jnp.clip(jnp.exp(math.log(3.0) - 2.3025851 * jax.random.uniform(keys[5], (SECTIONS, 2, HD), jnp.float32) ** levels(keys[5], (SECTIONS, 2, HD), ((0, 8),), -0.2, 0.2)), 0.3, 3.0),
        "w_out": normal_values(keys[6], (SECTIONS, HEADS * HD, D), (HEADS * HD + FF) ** -0.5, 0.0546875, ((0, 8), (1, 4))),
        "w_contract": normal_values(keys[7], (SECTIONS, FF, D), (HEADS * HD + FF) ** -0.5, 0.0546875, ((0, 8), (1, 4))),
        "stale_kv": draw_stale_kv(jax.random.fold_in(keys[9], 71), 0),
    }


def modulate(inputs, shift_row, scale_row):
    values = inputs.astype(jnp.float32)
    average = lax.optimization_barrier(jnp.mean(values, axis=-1, keepdims=True))
    centred = values - average
    variance = lax.optimization_barrier(jnp.mean(centred * centred, axis=-1, keepdims=True))
    normed = centred * lax.rsqrt(variance + 1e-06)
    return (normed * (1.0 + scale_row) + shift_row).astype(jnp.bfloat16)

def head_norm(values, gain_row):
    mean_square = lax.optimization_barrier(jnp.mean(values * values, axis=-1, keepdims=True))
    return (values * lax.rsqrt(mean_square + 1e-06) * gain_row).astype(jnp.bfloat16)

def single_block(inputs, modulation, w_qkv, w_expand, qk_gain, w_out, w_contract, stale_pair, patch_number):
    modulated = modulate(inputs, modulation[0], modulation[1])
    flat_weight = w_qkv.reshape(D, 3 * HEADS * HD)
    projected = jnp.dot(modulated, flat_weight, preferred_element_type=jnp.float32).reshape(PATCH, 3, HEADS, HD)
    expanded = jnp.dot(modulated, w_expand, preferred_element_type=jnp.float32)
    activated = jax.nn.gelu(expanded, approximate=True).astype(jnp.bfloat16)
    queries = head_norm(projected[:, 0], qk_gain[0])
    key_rows = head_norm(projected[:, 1], qk_gain[1])
    value_rows = projected[:, 2].astype(jnp.bfloat16)
    fresh_pair = jnp.stack([key_rows.reshape(PATCH, HEADS * HD), value_rows.reshape(PATCH, HEADS * HD)], axis=0)
    first_row = patch_number * PATCH
    merged = stale_pair.at[:, first_row:first_row + PATCH].set(fresh_pair)
    all_keys = merged[0].reshape(CONTEXT, HEADS, HD)
    all_values = merged[1].reshape(CONTEXT, HEADS, HD)
    scores = jnp.einsum('qhd,khd->hqk', queries.astype(jnp.float32), all_keys.astype(jnp.float32)) * HD ** (-0.5)
    highest = lax.optimization_barrier(jnp.max(scores, axis=-1, keepdims=True))
    weights = jnp.exp(scores - highest)
    totals = lax.optimization_barrier(jnp.sum(weights, axis=-1, keepdims=True))
    shares = (weights / totals).astype(jnp.bfloat16)
    mixed_rows = jnp.einsum('hqk,khd->qhd', shares.astype(jnp.float32), all_values.astype(jnp.float32)).astype(jnp.bfloat16)
    grouped = jnp.concatenate([mixed_rows.reshape(PATCH, N_SP, HEADS_DEV * HD), activated.reshape(PATCH, N_SP, FF_DEV)], axis=2)
    grouped_weight = jnp.concatenate([w_out.reshape(N_SP, HEADS_DEV * HD, D), w_contract.reshape(N_SP, FF_DEV, D)], axis=1)
    partials = jnp.einsum('pgc,gcd->gpd', grouped.astype(jnp.float32), grouped_weight.astype(jnp.float32)).astype(jnp.bfloat16)
    head_sum = lax.optimization_barrier(jnp.sum(partials.astype(jnp.float32), axis=0))
    result = (inputs.astype(jnp.float32) + modulation[2] * head_sum).astype(jnp.bfloat16)
    return (result, fresh_pair)

def reference(latents, in_flight, modulation, w_qkv, w_expand, qk_gain, w_out, w_contract, stale_kv):
    outputs = [[None] * MICRO for section_number in range(SECTIONS)]
    fresh_all = [[None] * MICRO for section_number in range(SECTIONS)]
    for tick_number in range(MICRO):
        for section_number in range(SECTIONS):
            if section_number == 0:
                inputs = latents[tick_number]
            elif tick_number == 0:
                inputs = in_flight[section_number]
            else:
                inputs = outputs[section_number - 1][tick_number - 1]
            patch_number = (tick_number - section_number) % MICRO
            result, fresh_pair = single_block(inputs, modulation[section_number], w_qkv[section_number], w_expand[section_number], qk_gain[section_number], w_out[section_number], w_contract[section_number], stale_kv[section_number], patch_number)
            outputs[section_number][tick_number] = result
            fresh_all[section_number][patch_number] = fresh_pair
    section_out = jnp.stack([jnp.stack(row_list, axis=0) for row_list in outputs], axis=0)
    fresh_kv = jnp.stack([jnp.stack(row_list, axis=0) for row_list in fresh_all], axis=0)
    return (section_out, fresh_kv)
```

```python
import functools

import jax
import jax.numpy as jnp
from jax import lax
from jax.experimental import pallas as pl
from jax.experimental.pallas import tpu as pltpu
from jax.sharding import PartitionSpec as P

F32 = jnp.float32
BF16 = jnp.bfloat16
TILE = 512
EARLY = 2
FLIGHT = 4
UNIT = 256
VMEM_LIMIT = 6 * 1024 * 1024


class Places:
    def __init__(self, width, head_cols, hidden):
        self.tile = min(TILE, head_cols)
        self.width, self.head_cols, self.hidden = width, head_cols, hidden
        self.head_starts = range(0, head_cols, self.tile)
        self.hidden_starts = range(0, hidden, self.tile)
        self.width_starts = range(0, width, self.tile)
        self.rows = [0, 0, 0]
        self.qkv = [[self.take(0, width) for _ in self.head_starts] for _ in range(3)]
        self.expand = [self.take(1, width) for _ in self.hidden_starts]
        self.back = [self.take(2, head_cols + hidden) for _ in self.width_starts]

    def take(self, array, rows):
        start = self.rows[array]
        self.rows[array] += rows
        return pl.ds(start, rows)

    def columns(self, start):
        return pl.ds(start, self.tile)


def dot(left, right):
    return jnp.dot(left, right, preferred_element_type=F32)


def head_norm(values, gain_row):
    mean_square = jnp.mean(values * values, axis=-1, keepdims=True)
    return (values * lax.rsqrt(mean_square + 1e-06) * gain_row).astype(BF16)


def gelu(values):
    inner = 0.7978845608028654 * (values + 0.044715 * values * values * values)
    return (0.5 * values * (1.0 + jnp.tanh(inner))).astype(BF16)


def attend(queries, all_keys, all_values, head_dim):
    scores = lax.dot_general(
        queries, all_keys, (((1,), (1,)), ((), ())), preferred_element_type=F32
    ) * head_dim ** (-0.5)
    highest = jnp.max(scores, axis=-1, keepdims=True)
    weights = jnp.exp(scores - highest)
    totals = jnp.sum(weights, axis=-1, keepdims=True)
    shares = (weights / totals).astype(BF16)
    return dot(shares, all_values).astype(BF16)


def in_vmem(array):
    return pltpu.with_memory_space_constraint(array, pltpu.VMEM)


def in_hbm(array):
    return pltpu.with_memory_space_constraint(array, pltpu.HBM)


def load_kernel(places, w_qkv, w_expand, stale, latents, qkv, expand, back, held_stale, later, sem):
    del back
    copies = [(stale, held_stale), (latents.at[pl.ds(1, later.shape[0])], later)]
    for part, tiles in enumerate(places.qkv):
        copies += [(w_qkv.at[part, :, places.columns(c)], qkv.at[to]) for c, to in zip(places.head_starts, tiles)]
    copies += [(w_expand.at[:, places.columns(places.hidden_starts[n])], expand.at[places.expand[n]]) for n in range(EARLY)]
    copies = [pltpu.make_async_copy(*pair, sem.at[i]) for i, pair in enumerate(copies)]
    for copy in copies:
        copy.start()
    for copy in copies:
        copy.wait()


def load(places, w_qkv, w_expand, stale, latents):
    arrays = (w_qkv, w_expand, stale, latents)
    later = (latents.shape[0] - 1, *latents.shape[1:])
    nbytes = 2 * (w_qkv.size + EARLY * places.width * places.tile)
    n_copies = 2 + 3 * len(places.head_starts) + EARLY
    return pl.pallas_call(
        functools.partial(load_kernel, places),
        out_shape=[
            *(pltpu.VMEM((n, places.tile), BF16) for n in places.rows),
            pltpu.VMEM(stale.shape, BF16),
            pltpu.VMEM(later, BF16),
        ],
        in_specs=[pl.BlockSpec(memory_space=pl.ANY)] * len(arrays),
        out_specs=[pl.BlockSpec(memory_space=pltpu.VMEM)] * 5,
        scratch_shapes=[pltpu.SemaphoreType.DMA((n_copies,))],
        cost_estimate=pl.CostEstimate(flops=0, bytes_accessed=2 * nbytes, transcendentals=0),
        compiler_params=pltpu.CompilerParams(vmem_limit_bytes=VMEM_LIMIT),
        name="load",
    )(*[in_hbm(a) for a in arrays])


def on_vectors(places, gain, weights, modulated, inner, fresh, context, modulate, keep_fresh, keep_partial, arrived):
    qkv, expand, back = weights
    head_dim, head_cols, tile = gain.shape[1], places.head_cols, places.tile
    modulate(slice(0, places.width))

    def project(part, start):
        return dot(modulated[...], qkv[places.qkv[part][start // tile], :])

    def heads(start):
        return [(slice(c, c + head_dim), slice(start + c, start + c + head_dim)) for c in range(0, tile, head_dim)]

    for start in places.head_starts:
        projected = project(1, start)
        for here, columns in heads(start):
            fresh[0, :, columns] = head_norm(projected[:, here], gain[1:2, :])
        fresh[1, :, start : start + tile] = project(2, start).astype(BF16)
    keep_fresh()
    for start in places.head_starts:
        projected = project(0, start)
        for here, columns in heads(start):
            queries = head_norm(projected[:, here], gain[0:1, :])
            inner[:, columns] = attend(queries, context[0, :, columns], context[1, :, columns], head_dim)
    for number, (start, to) in enumerate(zip(places.hidden_starts, places.expand)):
        arrived(number)
        inner[:, pl.ds(head_cols + start, tile)] = gelu(dot(modulated[...], expand[to, :]))
    for number, (start, to) in enumerate(zip(places.width_starts, places.back)):
        arrived(len(places.expand) + number)
        keep_partial(start, dot(inner[...], back[to, :]).astype(BF16))


def fits_units(places, head_dim, context_rows):
    depths = (places.width, places.head_cols + places.hidden)
    wide = places.tile == places.head_cols == 2 * UNIT == 4 * head_dim
    return wide and len(places.expand) > 3 and context_rows == UNIT and all(depth % UNIT == 0 for depth in depths)


def on_units(accumulators, places, gain, weights, modulated, inner, fresh, context, modulate, keep_fresh, keep_partial, arrived):
    qkv, expand, back = weights
    head_dim, tile = gain.shape[1], places.tile
    units = range(2)
    sets = (accumulators[0:2], accumulators[2:4])
    scored = accumulators[4:6]
    patch_rows = modulated.shape[0]

    def issue(left, right, rows, into, prepare=None):
        steps = rows.size // UNIT

        def push(k, unit):
            block = right[pl.ds(rows.start + k * UNIT, UNIT), unit * UNIT : (unit + 1) * UNIT]
            pltpu.matmul_push_rhs(block, k % 2, unit)

        for unit in units:
            push(0, unit)
        for k in range(steps):
            columns = slice(k * UNIT, (k + 1) * UNIT)
            if prepare is not None:
                prepare(columns)
            piece = left[:, columns]
            for unit in units:
                if k + 1 < steps:
                    push(k + 1, unit)
                pltpu.matmul_acc_lhs(into[unit], piece, load_staged_rhs=k % 2)

    def take(into):
        return [pltpu.matmul_pop(into[unit]) for unit in units]

    def normed(halves, gain_row):
        return [head_norm(half[:, c : c + head_dim], gain_row) for half in halves for c in range(0, UNIT, head_dim)]

    def keep_activated(number, halves):
        for unit in units:
            start = places.head_cols + number * tile + unit * UNIT
            inner[:, start : start + UNIT] = gelu(halves[unit])

    issue(modulated, qkv, places.qkv[1][0], sets[0], modulate)
    issue(modulated, qkv, places.qkv[2][0], sets[1])
    for h, keys in enumerate(normed(take(sets[0]), gain[1:2, :])):
        fresh[0, :, h * head_dim : (h + 1) * head_dim] = keys
    issue(modulated, qkv, places.qkv[0][0], sets[0])
    for unit, values in enumerate(take(sets[1])):
        fresh[1, :, unit * UNIT : (unit + 1) * UNIT] = values.astype(BF16)
    keep_fresh()

    expands = len(places.expand)
    issue(modulated, expand, places.expand[0], sets[1])
    queries = normed(take(sets[0]), gain[0:1, :])
    none = jnp.zeros((patch_rows, head_dim), BF16)
    for unit in units:
        one, other = queries[2 * unit : 2 * unit + 2]
        stacked = jnp.concatenate(
            [jnp.concatenate([one, none], axis=1), jnp.concatenate([none, other], axis=1)], axis=0
        )
        pltpu.matmul_push_rhs(context[0, :, unit * UNIT : (unit + 1) * UNIT], 0, unit, transpose=True)
        pltpu.matmul_acc_lhs(scored[unit], stacked, load_staged_rhs=0)
    for number in range(1, expands):
        arrived(number)
        issue(modulated, expand, places.expand[number], sets[(number + 1) % 2])
        keep_activated(number - 1, take(sets[number % 2]))
        if number == 1:
            shares = []
            for unit in units:
                scores = pltpu.matmul_pop(scored[unit]) * head_dim ** (-0.5)
                highest = jnp.max(scores, axis=-1, keepdims=True)
                exps = jnp.exp(scores - highest)
                shares.append((exps / jnp.sum(exps, axis=-1, keepdims=True)).astype(BF16))
        if number == 2:
            for unit in units:
                pltpu.matmul_push_rhs(context[1, :, unit * UNIT : (unit + 1) * UNIT], 0, unit)
                pltpu.matmul_acc_lhs(scored[unit], shares[unit], load_staged_rhs=0)
        if number == 3:
            for unit in units:
                both = pltpu.matmul_pop(scored[unit]).astype(BF16)
                start = unit * UNIT
                inner[:, start : start + head_dim] = both[:patch_rows, :head_dim]
                inner[:, start + head_dim : start + UNIT] = both[patch_rows:, head_dim:]
    keep_activated(expands - 1, take(sets[expands % 2]))

    def keep(number):
        for unit, total in enumerate(take(sets[number % 2])):
            keep_partial(number * tile + unit * UNIT, total.astype(BF16))

    for number, rows in enumerate(places.back):
        arrived(expands + number)
        issue(inner, back, rows, sets[number % 2])
        if number > 0:
            keep(number - 1)
    keep(len(places.back) - 1)


def block_kernel(tick, micro, group, places, accumulators, *refs):
    refs = list(refs)
    n_chunks = group if tick == 0 else 2
    chunks = refs[:n_chunks]
    modulation, gain, stale, qkv, expand, back = refs[n_chunks : n_chunks + 6]
    refs = refs[n_chunks + 6 :]
    modulated, inner, fresh, context, sems = refs[-5:]
    refs = refs[:-5]
    patch_rows = modulated.shape[0]
    half = patch_rows // 2
    rows = patch_rows // group
    me = lax.axis_index("sp")
    core, order = jnp.bitwise_and(me, 1), jnp.right_shift(me, 1)
    copies, loads = [], []
    if tick == 0:
        w_expand, w_out, w_contract = refs[:3]
        partials, fresh_all, expand, back, entered = refs[3:5], *refs[5:9]
        tiles = []
        for number in range(EARLY, len(places.expand)):
            columns = places.columns(places.hidden_starts[number])
            tiles.append([(w_expand.at[:, columns], expand.at[places.expand[number]])])
        for start, to in zip(places.width_starts, places.back):
            columns = places.columns(start)
            tiles.append(
                [
                    (w_out.at[:, columns], back.at[pl.ds(to.start, places.head_cols)]),
                    (w_contract.at[:, columns], back.at[pl.ds(to.start + places.head_cols, places.hidden)]),
                ]
            )
        number = group
        for pieces in tiles:
            loads.append([pltpu.make_async_copy(*piece, sems.at[number + i]) for i, piece in enumerate(pieces)])
            number += len(pieces)
        for tile in loads[:FLIGHT]:
            for copy in tile:
                copy.start()
    else:
        result = refs[0]
        refs = refs[1 + min(tick, 2) :]
        partials, fresh_all, section_out = refs[:2], refs[2], refs[3]
        copies.append(pltpu.make_async_copy(result, section_out.at[tick - 1], sems.at[group]))
        copies[-1].start()
    patch = lax.rem(tick - lax.axis_index("section") + micro * lax.axis_size("section"), micro)
    place = pl.ds(pl.multiple_of(patch * patch_rows, patch_rows), patch_rows)

    stats = []
    for d, chunk in enumerate(chunks):
        inputs = chunk[...]
        if tick == 0:
            here = pl.multiple_of(jnp.bitwise_xor(order, d >> 1) * rows, rows)
            if d % 2 == 0:
                entered[pl.ds(here, rows), :] = inputs
            here = pl.multiple_of(here + d % 2 * half, rows)
        else:
            here = d * half
        values = inputs.astype(F32)
        average = jnp.mean(values, axis=-1, keepdims=True)
        centred = values - average
        variance = jnp.mean(centred * centred, axis=-1, keepdims=True)
        stats.append((chunk, pl.ds(here, inputs.shape[0]), average, lax.rsqrt(variance + 1e-06)))

    def modulate(columns):
        scale_row, shift_row = 1.0 + modulation[1, :, columns], modulation[0, :, columns]
        for chunk, here, average, inverse in stats:
            normed = (chunk[:, columns].astype(F32) - average) * inverse
            modulated[here, columns] = (normed * scale_row + shift_row).astype(BF16)

    context[...] = stale[...]

    def keep_fresh():
        context[:, place, :] = fresh[...]
        for d in range(group):
            owner = 2 * (d % (group // 2)) + jnp.bitwise_xor(core, d // (group // 2))
            copies.append(
                pltpu.make_async_copy(
                    fresh.at[:, pl.ds(d * rows, rows), :],
                    fresh_all.at[patch, :, pl.ds(pl.multiple_of(owner * rows, rows), rows), :],
                    sems.at[d],
                )
            )
            copies[-1].start()

    def keep_partial(start, total):
        for d in range(2):
            partials[d][:, pl.ds(start, total.shape[1])] = total[d * half : (d + 1) * half]

    def arrived(number):
        if tick > 0 or number < EARLY:
            return
        number -= EARLY
        for copy in loads[number]:
            copy.wait()
        for tile in loads[number + FLIGHT : number + FLIGHT + 1]:
            for copy in tile:
                copy.start()

    shared = (places, gain, (qkv, expand, back), modulated, inner, fresh, context, modulate, keep_fresh, keep_partial, arrived)

    def work(*into):
        if into:
            on_units(into, *shared)
        else:
            on_vectors(*shared)
        for copy in copies:
            copy.wait()

    pl.run_scoped(work, *accumulators)


def block(tick, micro, group, places, chunks, modulation, gain, stale, held, weights, result, section_out, fresh_all):
    width = chunks[0].shape[1]
    patch_rows = sum(chunk.shape[0] for chunk in chunks)
    half = jax.ShapeDtypeStruct((patch_rows // 2, width), BF16)
    vmem = pl.BlockSpec(memory_space=pltpu.VMEM)
    anywhere = pl.BlockSpec(memory_space=pl.ANY)
    out_shape = [pltpu.VMEM(half.shape, BF16)] * 2
    out_shape.append(jax.ShapeDtypeStruct((micro, 2, patch_rows, places.head_cols), BF16))
    out_specs = [vmem] * 2 + [anywhere]
    operands = [in_vmem(x) for x in (*chunks, modulation, gain, stale, *held)]
    in_specs = [vmem] * len(operands)
    aliases = {}
    n_sems = group + 1
    if tick == 0:
        aliases = {len(operands) - 2: 3, len(operands) - 1: 4}
        operands += [in_hbm(w) for w in weights]
        in_specs += [anywhere] * len(weights)
        out_shape += [pltpu.VMEM(shape, BF16) for shape in (held[1].shape, held[2].shape, half.shape)]
        out_specs += [vmem] * 3
        n_sems = group + len(places.expand) - EARLY + 2 * len(places.back)
    else:
        operands.append(in_vmem(result))
        in_specs.append(vmem)
        out_shape.append(jax.ShapeDtypeStruct((micro, patch_rows // group, width), BF16))
        out_specs.append(anywhere)
        for number, array in enumerate((fresh_all, section_out)):
            if array is not None:
                aliases[len(operands)] = 2 + number
                operands.append(in_hbm(array))
                in_specs.append(anywhere)
    accumulators = []
    if fits_units(places, gain.shape[1], stale.shape[1]):
        accumulators = [pltpu.ACC(unit)((patch_rows, UNIT), F32) for _ in range(2) for unit in range(2)]
        accumulators += [pltpu.ACC(unit)((2 * patch_rows, UNIT), F32) for unit in range(2)]
    return pl.pallas_call(
        functools.partial(block_kernel, tick, micro, group, places, accumulators),
        out_shape=out_shape,
        in_specs=in_specs,
        out_specs=out_specs,
        scratch_shapes=[
            pltpu.VMEM((patch_rows, width), BF16),
            pltpu.VMEM((patch_rows, places.head_cols + places.hidden), BF16),
            pltpu.VMEM((2, patch_rows, places.head_cols), BF16),
            pltpu.VMEM(stale.shape, BF16),
            pltpu.SemaphoreType.DMA((n_sems,)),
        ],
        input_output_aliases=aliases,
        cost_estimate=pl.CostEstimate(
            flops=2 * patch_rows * places.tile * sum(places.rows),
            bytes_accessed=2 * places.tile * sum(places.rows),
            transcendentals=patch_rows * places.hidden,
        ),
        compiler_params=pltpu.CompilerParams(vmem_limit_bytes=VMEM_LIMIT),
        name="block",
    )(*operands)


def small(kernel, name, out_shapes, operands):
    vmem = pl.BlockSpec(memory_space=pltpu.VMEM)
    return pl.pallas_call(
        kernel,
        out_shape=[pltpu.VMEM(shape, BF16) for shape in out_shapes],
        in_specs=[vmem] * len(operands),
        out_specs=[vmem] * len(out_shapes),
        compiler_params=pltpu.CompilerParams(vmem_limit_bytes=VMEM_LIMIT),
        name=name,
    )(*[in_vmem(x) for x in operands])


def place_of(distance, rows):
    order = jnp.right_shift(lax.axis_index("sp"), 1)
    return pl.ds(pl.multiple_of(jnp.bitwise_xor(order, distance) * rows, rows), rows)


def add_pair_kernel(one, other, *refs):
    chips = lax.axis_size("sp") // 2
    for e, out in enumerate(refs[-chips:]):
        rows = place_of(e, out.shape[0])
        out[...] = (one[rows, :].astype(F32) + other[rows, :].astype(F32)).astype(BF16)


def add_pair(one, other, chips):
    shape = (one.shape[0] // chips, one.shape[1])
    return small(add_pair_kernel, "add_pair", [shape] * chips, (one, other))


def finish(parts, inputs, modulation):
    total = parts[0][...].astype(F32)
    for part in parts[1:]:
        total = total + part[...].astype(F32)
    entered = inputs[place_of(0, total.shape[0]), :]
    return (entered.astype(F32) + modulation[2] * total).astype(BF16)


def finish_kernel(tick, *refs):
    *parts, inputs, modulation, later, out, leaving = refs
    result = finish(parts, inputs, modulation)
    out[...] = result
    is_last = lax.axis_index("section") == lax.axis_size("section") - 1
    leaving[...] = jnp.where(is_last, later[tick], result)


def last_kernel(tick, *refs):
    *parts, inputs, modulation, _, section_out, held, sem = refs
    held[...] = finish(parts, inputs, modulation)
    copy = pltpu.make_async_copy(held, section_out.at[tick], sem)
    copy.start()
    copy.wait()


def finish_last(tick, parts, inputs, modulation, section_out):
    vmem = pl.BlockSpec(memory_space=pltpu.VMEM)
    anywhere = pl.BlockSpec(memory_space=pl.ANY)
    operands = [in_vmem(x) for x in (*parts, inputs, modulation)]
    return pl.pallas_call(
        functools.partial(last_kernel, tick),
        out_shape=jax.ShapeDtypeStruct(section_out.shape, BF16),
        in_specs=[vmem] * len(operands) + [anywhere],
        out_specs=anywhere,
        scratch_shapes=[pltpu.VMEM(parts[0].shape, BF16), pltpu.SemaphoreType.DMA],
        input_output_aliases={len(operands): 0},
        compiler_params=pltpu.CompilerParams(vmem_limit_bytes=VMEM_LIMIT),
        name="finish_last",
    )(*operands, in_hbm(section_out))


def enter_kernel(*refs):
    *passed, out = refs
    for e, chunk in enumerate(passed):
        out[place_of(e, chunk.shape[0]), :] = chunk[...]


def swap(rows, distance):
    group = lax.axis_size("sp")
    if distance == 0:
        return rows
    return lax.ppermute(rows, "sp", [(i, i ^ distance) for i in range(group)])


def to_next_section(rows, distance):
    sections, group = lax.axis_size("section"), lax.axis_size("sp")
    route = [
        (s * group + i, (s + 1) % sections * group + (i ^ distance)) for s in range(sections) for i in range(group)
    ]
    return lax.ppermute(rows, ("section", "sp"), route)


def local(latents, in_flight, modulation, w_qkv, w_expand, qk_gain, w_out, w_contract, stale_kv):
    group = lax.axis_size("sp")
    micro = latents.shape[0]
    start = jnp.where(lax.axis_index("section") == 0, latents[0], in_flight[0])
    chunks = [swap(start, d) for d in range(group)]
    rows_modulation = jnp.transpose(modulation, (1, 0, 2))
    places = Places(w_qkv.shape[1], w_qkv.shape[3], w_expand.shape[2])
    qkv, expand, back, stale, later = load(
        places, jnp.transpose(w_qkv[0], (1, 0, 2)), w_expand[0], stale_kv[0], latents
    )
    weights = (w_expand[0], w_out[0], w_contract[0])
    chips = group // 2
    result, fresh_all, section_out = None, None, None
    for tick in range(micro):
        held = (qkv, expand, back)
        kept, sent, fresh_all, *others = block(
            tick, micro, group, places, chunks, rows_modulation, qk_gain[0], stale, held, weights, result, section_out, fresh_all
        )
        if tick == 0:
            expand, back, inputs = others
        else:
            (section_out,) = others
        sums = add_pair(kept, swap(sent, 1), chips)
        parts = [swap(sums[e], 2 * e) for e in range(chips)]
        if tick == micro - 1:
            section_out = finish_last(tick, parts, inputs, rows_modulation, section_out)
        else:
            result, leaving = small(
                functools.partial(finish_kernel, tick),
                "finish",
                [parts[0].shape] * 2,
                (*parts, inputs, rows_modulation, later),
            )
            passed = [to_next_section(leaving, 2 * e) for e in range(chips)]
            (inputs,) = small(enter_kernel, "enter", [inputs.shape], passed)
            chunks = [inputs, swap(inputs, 1)]
    return (section_out[None], fresh_all[None])


def solution(mesh):
    placed = (
        P(None, "sp", None),
        P("section", "sp", None),
        P("section", None, None),
        P("section", None, None, "sp"),
        P("section", None, "sp"),
        P("section", None, None),
        P("section", "sp", None),
        P("section", "sp", None),
        P("section", None, None, "sp"),
    )
    return jax.shard_map(
        local,
        mesh=mesh,
        in_specs=placed,
        out_specs=(P("section", None, "sp", None), P("section", None, None, None, "sp")),
        check_vma=False,
    )
```

```python
import functools

import jax
import jax.numpy as jnp
from jax import lax
from jax.experimental import pallas as pl
from jax.experimental.pallas import tpu as pltpu
from jax.sharding import PartitionSpec as P

F32 = jnp.float32
BF16 = jnp.bfloat16
TILE = 512
EARLY = 2
FLIGHT = 4
UNIT = 256
VMEM_LIMIT = 6 * 1024 * 1024


class Places:
    def __init__(self, width, head_cols, hidden):
        self.tile = min(TILE, head_cols)
        self.width, self.head_cols, self.hidden = width, head_cols, hidden
        self.head_starts = range(0, head_cols, self.tile)
        self.hidden_starts = range(0, hidden, self.tile)
        self.width_starts = range(0, width, self.tile)
        self.rows = [0, 0, 0]
        self.qkv = [[self.take(0, width) for _ in self.head_starts] for _ in range(3)]
        self.expand = [self.take(1, width) for _ in self.hidden_starts]
        self.back = [self.take(2, head_cols + hidden) for _ in self.width_starts]

    def take(self, array, rows):
        start = self.rows[array]
        self.rows[array] += rows
        return pl.ds(start, rows)

    def columns(self, start):
        return pl.ds(start, self.tile)


def dot(left, right):
    return jnp.dot(left, right, preferred_element_type=F32)


def head_norm(values, gain_row):
    mean_square = jnp.mean(values * values, axis=-1, keepdims=True)
    return (values * lax.rsqrt(mean_square + 1e-06) * gain_row).astype(BF16)


def gelu(values):
    inner = 0.7978845608028654 * (values + 0.044715 * values * values * values)
    return (0.5 * values * (1.0 + jnp.tanh(inner))).astype(BF16)


def attend(queries, all_keys, all_values, head_dim):
    scores = lax.dot_general(
        queries, all_keys, (((1,), (1,)), ((), ())), preferred_element_type=F32
    ) * head_dim ** (-0.5)
    highest = jnp.max(scores, axis=-1, keepdims=True)
    weights = jnp.exp(scores - highest)
    totals = jnp.sum(weights, axis=-1, keepdims=True)
    shares = (weights / totals).astype(BF16)
    return dot(shares, all_values).astype(BF16)


def in_vmem(array):
    return pltpu.with_memory_space_constraint(array, pltpu.VMEM)


def in_hbm(array):
    return pltpu.with_memory_space_constraint(array, pltpu.HBM)


def load_kernel(places, w_qkv, w_expand, stale, latents, qkv, expand, back, held_stale, later, sem):
    del back
    copies = [(stale, held_stale), (latents.at[pl.ds(1, later.shape[0])], later)]
    for part, tiles in enumerate(places.qkv):
        copies += [(w_qkv.at[part, :, places.columns(c)], qkv.at[to]) for c, to in zip(places.head_starts, tiles)]
    copies += [(w_expand.at[:, places.columns(places.hidden_starts[n])], expand.at[places.expand[n]]) for n in range(EARLY)]
    copies = [pltpu.make_async_copy(*pair, sem.at[i]) for i, pair in enumerate(copies)]
    for copy in copies:
        copy.start()
    for copy in copies:
        copy.wait()


def load(places, w_qkv, w_expand, stale, latents):
    arrays = (w_qkv, w_expand, stale, latents)
    later = (latents.shape[0] - 1, *latents.shape[1:])
    nbytes = 2 * (w_qkv.size + EARLY * places.width * places.tile)
    n_copies = 2 + 3 * len(places.head_starts) + EARLY
    return pl.pallas_call(
        functools.partial(load_kernel, places),
        out_shape=[
            *(pltpu.VMEM((n, places.tile), BF16) for n in places.rows),
            pltpu.VMEM(stale.shape, BF16),
            pltpu.VMEM(later, BF16),
        ],
        in_specs=[pl.BlockSpec(memory_space=pl.ANY)] * len(arrays),
        out_specs=[pl.BlockSpec(memory_space=pltpu.VMEM)] * 5,
        scratch_shapes=[pltpu.SemaphoreType.DMA((n_copies,))],
        cost_estimate=pl.CostEstimate(flops=0, bytes_accessed=2 * nbytes, transcendentals=0),
        compiler_params=pltpu.CompilerParams(vmem_limit_bytes=VMEM_LIMIT),
        name="load",
    )(*[in_hbm(a) for a in arrays])


def on_vectors(places, gain, weights, modulated, inner, fresh, context, modulate, keep_fresh, keep_partial, arrived):
    qkv, expand, back = weights
    head_dim, head_cols, tile = gain.shape[1], places.head_cols, places.tile
    modulate(slice(0, places.width))

    def project(part, start):
        return dot(modulated[...], qkv[places.qkv[part][start // tile], :])

    def heads(start):
        return [(slice(c, c + head_dim), slice(start + c, start + c + head_dim)) for c in range(0, tile, head_dim)]

    for start in places.head_starts:
        projected = project(1, start)
        for here, columns in heads(start):
            fresh[0, :, columns] = head_norm(projected[:, here], gain[1:2, :])
        fresh[1, :, start : start + tile] = project(2, start).astype(BF16)
    keep_fresh()
    for start in places.head_starts:
        projected = project(0, start)
        for here, columns in heads(start):
            queries = head_norm(projected[:, here], gain[0:1, :])
            inner[:, columns] = attend(queries, context[0, :, columns], context[1, :, columns], head_dim)
    for number, (start, to) in enumerate(zip(places.hidden_starts, places.expand)):
        arrived(number)
        inner[:, pl.ds(head_cols + start, tile)] = gelu(dot(modulated[...], expand[to, :]))
    for number, (start, to) in enumerate(zip(places.width_starts, places.back)):
        arrived(len(places.expand) + number)
        keep_partial(start, dot(inner[...], back[to, :]).astype(BF16))


def fits_units(places, head_dim, context_rows):
    depths = (places.width, places.head_cols + places.hidden)
    wide = places.tile == places.head_cols == 2 * UNIT == 4 * head_dim
    return wide and len(places.expand) > 3 and context_rows == UNIT and all(depth % UNIT == 0 for depth in depths)


def on_units(accumulators, places, gain, weights, modulated, inner, fresh, context, modulate, keep_fresh, keep_partial, arrived):
    qkv, expand, back = weights
    head_dim, tile = gain.shape[1], places.tile
    units = range(2)
    sets = (accumulators[0:2], accumulators[2:4])
    scored = accumulators[4:6]
    patch_rows = modulated.shape[0]

    def issue(left, right, rows, into, prepare=None):
        steps = rows.size // UNIT

        def push(k, unit):
            block = right[pl.ds(rows.start + k * UNIT, UNIT), unit * UNIT : (unit + 1) * UNIT]
            pltpu.matmul_push_rhs(block, k % 2, unit)

        for unit in units:
            push(0, unit)
        for k in range(steps):
            columns = slice(k * UNIT, (k + 1) * UNIT)
            if prepare is not None:
                prepare(columns)
            piece = left[:, columns]
            for unit in units:
                if k + 1 < steps:
                    push(k + 1, unit)
                pltpu.matmul_acc_lhs(into[unit], piece, load_staged_rhs=k % 2)

    def take(into):
        return [pltpu.matmul_pop(into[unit]) for unit in units]

    def normed(halves, gain_row):
        return [head_norm(half[:, c : c + head_dim], gain_row) for half in halves for c in range(0, UNIT, head_dim)]

    def keep_activated(number, halves):
        for unit in units:
            start = places.head_cols + number * tile + unit * UNIT
            inner[:, start : start + UNIT] = gelu(halves[unit])

    issue(modulated, qkv, places.qkv[1][0], sets[0], modulate)
    issue(modulated, qkv, places.qkv[2][0], sets[1])
    for h, keys in enumerate(normed(take(sets[0]), gain[1:2, :])):
        fresh[0, :, h * head_dim : (h + 1) * head_dim] = keys
    issue(modulated, qkv, places.qkv[0][0], sets[0])
    for unit, values in enumerate(take(sets[1])):
        fresh[1, :, unit * UNIT : (unit + 1) * UNIT] = values.astype(BF16)
    keep_fresh()

    expands = len(places.expand)
    issue(modulated, expand, places.expand[0], sets[1])
    queries = normed(take(sets[0]), gain[0:1, :])
    none = jnp.zeros((patch_rows, head_dim), BF16)
    for unit in units:
        one, other = queries[2 * unit : 2 * unit + 2]
        stacked = jnp.concatenate(
            [jnp.concatenate([one, none], axis=1), jnp.concatenate([none, other], axis=1)], axis=0
        )
        pltpu.matmul_push_rhs(context[0, :, unit * UNIT : (unit + 1) * UNIT], 0, unit, transpose=True)
        pltpu.matmul_acc_lhs(scored[unit], stacked, load_staged_rhs=0)
    for number in range(1, expands):
        arrived(number)
        issue(modulated, expand, places.expand[number], sets[(number + 1) % 2])
        keep_activated(number - 1, take(sets[number % 2]))
        if number == 1:
            shares = []
            for unit in units:
                scores = pltpu.matmul_pop(scored[unit]) * head_dim ** (-0.5)
                highest = jnp.max(scores, axis=-1, keepdims=True)
                exps = jnp.exp(scores - highest)
                shares.append((exps / jnp.sum(exps, axis=-1, keepdims=True)).astype(BF16))
        if number == 2:
            for unit in units:
                pltpu.matmul_push_rhs(context[1, :, unit * UNIT : (unit + 1) * UNIT], 0, unit)
                pltpu.matmul_acc_lhs(scored[unit], shares[unit], load_staged_rhs=0)
        if number == 3:
            for unit in units:
                both = pltpu.matmul_pop(scored[unit]).astype(BF16)
                start = unit * UNIT
                inner[:, start : start + head_dim] = both[:patch_rows, :head_dim]
                inner[:, start + head_dim : start + UNIT] = both[patch_rows:, head_dim:]
    keep_activated(expands - 1, take(sets[expands % 2]))

    def keep(number):
        for unit, total in enumerate(take(sets[number % 2])):
            keep_partial(number * tile + unit * UNIT, total.astype(BF16))

    for number, rows in enumerate(places.back):
        arrived(expands + number)
        issue(inner, back, rows, sets[number % 2])
        if number > 0:
            keep(number - 1)
    keep(len(places.back) - 1)


def block_kernel(tick, micro, group, places, accumulators, *refs):
    refs = list(refs)
    n_chunks = group if tick == 0 else 2
    chunks = refs[:n_chunks]
    modulation, gain, stale, qkv, expand, back = refs[n_chunks : n_chunks + 6]
    refs = refs[n_chunks + 6 :]
    modulated, inner, fresh, context, sems = refs[-5:]
    refs = refs[:-5]
    patch_rows = modulated.shape[0]
    half = patch_rows // 2
    rows = patch_rows // group
    me = lax.axis_index("sp")
    core, order = jnp.bitwise_and(me, 1), jnp.right_shift(me, 1)
    copies, loads = [], []
    if tick == 0:
        w_expand, w_out, w_contract = refs[:3]
        partials, fresh_all, expand, back, entered = refs[3:5], *refs[5:9]
        tiles = []
        for number in range(EARLY, len(places.expand)):
            columns = places.columns(places.hidden_starts[number])
            tiles.append([(w_expand.at[:, columns], expand.at[places.expand[number]])])
        for start, to in zip(places.width_starts, places.back):
            columns = places.columns(start)
            tiles.append(
                [
                    (w_out.at[:, columns], back.at[pl.ds(to.start, places.head_cols)]),
                    (w_contract.at[:, columns], back.at[pl.ds(to.start + places.head_cols, places.hidden)]),
                ]
            )
        number = group
        for pieces in tiles:
            loads.append([pltpu.make_async_copy(*piece, sems.at[number + i]) for i, piece in enumerate(pieces)])
            number += len(pieces)
        for tile in loads[:FLIGHT]:
            for copy in tile:
                copy.start()
    else:
        result = refs[0]
        refs = refs[1 + min(tick, 2) :]
        partials, fresh_all, section_out = refs[:2], refs[2], refs[3]
        copies.append(pltpu.make_async_copy(result, section_out.at[tick - 1], sems.at[group]))
        copies[-1].start()
    patch = lax.rem(tick - lax.axis_index("section") + micro * lax.axis_size("section"), micro)
    place = pl.ds(pl.multiple_of(patch * patch_rows, patch_rows), patch_rows)

    stats = []
    for d, chunk in enumerate(chunks):
        inputs = chunk[...]
        if tick == 0:
            here = pl.multiple_of(jnp.bitwise_xor(order, d >> 1) * rows, rows)
            if d % 2 == 0:
                entered[pl.ds(here, rows), :] = inputs
            here = pl.multiple_of(here + d % 2 * half, rows)
        else:
            here = d * half
        values = inputs.astype(F32)
        average = jnp.mean(values, axis=-1, keepdims=True)
        centred = values - average
        variance = jnp.mean(centred * centred, axis=-1, keepdims=True)
        stats.append((chunk, pl.ds(here, inputs.shape[0]), average, lax.rsqrt(variance + 1e-06)))

    def modulate(columns):
        scale_row, shift_row = 1.0 + modulation[1, :, columns], modulation[0, :, columns]
        for chunk, here, average, inverse in stats:
            normed = (chunk[:, columns].astype(F32) - average) * inverse
            modulated[here, columns] = (normed * scale_row + shift_row).astype(BF16)

    context[...] = stale[...]

    def keep_fresh():
        context[:, place, :] = fresh[...]
        for d in range(group):
            owner = 2 * (d % (group // 2)) + jnp.bitwise_xor(core, d // (group // 2))
            copies.append(
                pltpu.make_async_copy(
                    fresh.at[:, pl.ds(d * rows, rows), :],
                    fresh_all.at[patch, :, pl.ds(pl.multiple_of(owner * rows, rows), rows), :],
                    sems.at[d],
                )
            )
            copies[-1].start()

    def keep_partial(start, total):
        for d in range(2):
            partials[d][:, pl.ds(start, total.shape[1])] = total[d * half : (d + 1) * half]

    def arrived(number):
        if tick > 0 or number < EARLY:
            return
        number -= EARLY
        for copy in loads[number]:
            copy.wait()
        for tile in loads[number + FLIGHT : number + FLIGHT + 1]:
            for copy in tile:
                copy.start()

    shared = (places, gain, (qkv, expand, back), modulated, inner, fresh, context, modulate, keep_fresh, keep_partial, arrived)

    def work(*into):
        if into:
            on_units(into, *shared)
        else:
            on_vectors(*shared)
        for copy in copies:
            copy.wait()

    pl.run_scoped(work, *accumulators)


def block(tick, micro, group, places, chunks, modulation, gain, stale, held, weights, result, section_out, fresh_all):
    width = chunks[0].shape[1]
    patch_rows = sum(chunk.shape[0] for chunk in chunks)
    half = jax.ShapeDtypeStruct((patch_rows // 2, width), BF16)
    vmem = pl.BlockSpec(memory_space=pltpu.VMEM)
    anywhere = pl.BlockSpec(memory_space=pl.ANY)
    out_shape = [pltpu.VMEM(half.shape, BF16)] * 2
    out_shape.append(jax.ShapeDtypeStruct((micro, 2, patch_rows, places.head_cols), BF16))
    out_specs = [vmem] * 2 + [anywhere]
    operands = [in_vmem(x) for x in (*chunks, modulation, gain, stale, *held)]
    in_specs = [vmem] * len(operands)
    aliases = {}
    n_sems = group + 1
    if tick == 0:
        aliases = {len(operands) - 2: 3, len(operands) - 1: 4}
        operands += [in_hbm(w) for w in weights]
        in_specs += [anywhere] * len(weights)
        out_shape += [pltpu.VMEM(shape, BF16) for shape in (held[1].shape, held[2].shape, half.shape)]
        out_specs += [vmem] * 3
        n_sems = group + len(places.expand) - EARLY + 2 * len(places.back)
    else:
        operands.append(in_vmem(result))
        in_specs.append(vmem)
        out_shape.append(jax.ShapeDtypeStruct((micro, patch_rows // group, width), BF16))
        out_specs.append(anywhere)
        for number, array in enumerate((fresh_all, section_out)):
            if array is not None:
                aliases[len(operands)] = 2 + number
                operands.append(in_hbm(array))
                in_specs.append(anywhere)
    accumulators = []
    if fits_units(places, gain.shape[1], stale.shape[1]):
        accumulators = [pltpu.ACC(unit)((patch_rows, UNIT), F32) for _ in range(2) for unit in range(2)]
        accumulators += [pltpu.ACC(unit)((2 * patch_rows, UNIT), F32) for unit in range(2)]
    return pl.pallas_call(
        functools.partial(block_kernel, tick, micro, group, places, accumulators),
        out_shape=out_shape,
        in_specs=in_specs,
        out_specs=out_specs,
        scratch_shapes=[
            pltpu.VMEM((patch_rows, width), BF16),
            pltpu.VMEM((patch_rows, places.head_cols + places.hidden), BF16),
            pltpu.VMEM((2, patch_rows, places.head_cols), BF16),
            pltpu.VMEM(stale.shape, BF16),
            pltpu.SemaphoreType.DMA((n_sems,)),
        ],
        input_output_aliases=aliases,
        cost_estimate=pl.CostEstimate(
            flops=2 * patch_rows * places.tile * sum(places.rows),
            bytes_accessed=2 * places.tile * sum(places.rows),
            transcendentals=patch_rows * places.hidden,
        ),
        compiler_params=pltpu.CompilerParams(vmem_limit_bytes=VMEM_LIMIT),
        name="block",
    )(*operands)


def small(kernel, name, out_shapes, operands, unused=()):
    vmem = pl.BlockSpec(memory_space=pltpu.VMEM)
    return pl.pallas_call(
        kernel,
        out_shape=[pltpu.VMEM(shape, BF16) for shape in out_shapes],
        in_specs=[vmem] * len(operands) + [pl.BlockSpec(memory_space=pl.ANY)] * len(unused),
        out_specs=[vmem] * len(out_shapes),
        compiler_params=pltpu.CompilerParams(vmem_limit_bytes=VMEM_LIMIT),
        name=name,
    )(*[in_vmem(x) for x in operands], *unused)


def place_of(distance, rows):
    order = jnp.right_shift(lax.axis_index("sp"), 1)
    return pl.ds(pl.multiple_of(jnp.bitwise_xor(order, distance) * rows, rows), rows)


def add_pair_kernel(one, other, *refs):
    chips = lax.axis_size("sp") // 2
    for e, out in enumerate(refs[-chips:]):
        rows = place_of(e, out.shape[0])
        out[...] = (one[rows, :].astype(F32) + other[rows, :].astype(F32)).astype(BF16)


def add_pair(one, other, chips, unused):
    shape = (one.shape[0] // chips, one.shape[1])
    return small(add_pair_kernel, "add_pair", [shape] * chips, (one, other), unused)


def finish(parts, inputs, modulation):
    total = parts[0][...].astype(F32)
    for part in parts[1:]:
        total = total + part[...].astype(F32)
    entered = inputs[place_of(0, total.shape[0]), :]
    return (entered.astype(F32) + modulation[2] * total).astype(BF16)


def finish_kernel(*refs):
    *parts, inputs, modulation, out = refs
    out[...] = finish(parts, inputs, modulation)


def last_kernel(tick, *refs):
    *parts, inputs, modulation, _, section_out, held, sem = refs
    held[...] = finish(parts, inputs, modulation)
    copy = pltpu.make_async_copy(held, section_out.at[tick], sem)
    copy.start()
    copy.wait()


def finish_last(tick, parts, inputs, modulation, section_out):
    vmem = pl.BlockSpec(memory_space=pltpu.VMEM)
    anywhere = pl.BlockSpec(memory_space=pl.ANY)
    operands = [in_vmem(x) for x in (*parts, inputs, modulation)]
    return pl.pallas_call(
        functools.partial(last_kernel, tick),
        out_shape=jax.ShapeDtypeStruct(section_out.shape, BF16),
        in_specs=[vmem] * len(operands) + [anywhere],
        out_specs=anywhere,
        scratch_shapes=[pltpu.VMEM(parts[0].shape, BF16), pltpu.SemaphoreType.DMA],
        input_output_aliases={len(operands): 0},
        compiler_params=pltpu.CompilerParams(vmem_limit_bytes=VMEM_LIMIT),
        name="finish_last",
    )(*operands, in_hbm(section_out))


def enter_kernel(tick, *refs):
    chips = len(refs) // 2
    passed, early, out = refs[:chips], refs[chips : 2 * chips], refs[-1]
    rows = passed[0].shape[0]
    is_first = lax.axis_index("section") == 0
    for e in range(chips):
        out[place_of(e, rows), :] = jnp.where(is_first, early[e][tick], passed[e][...])


def swap(rows, distance):
    group = lax.axis_size("sp")
    if distance == 0:
        return rows
    return lax.ppermute(rows, "sp", [(i, i ^ distance) for i in range(group)])


def to_next_section(rows, distance):
    sections, group = lax.axis_size("section"), lax.axis_size("sp")
    route = [(s * group + i, (s + 1) * group + (i ^ distance)) for s in range(sections - 1) for i in range(group)]
    route += [((sections - 1) * group + i, i) for i in range(group)]
    return lax.ppermute(rows, ("section", "sp"), route)


def local(latents, in_flight, modulation, w_qkv, w_expand, qk_gain, w_out, w_contract, stale_kv):
    group = lax.axis_size("sp")
    micro = latents.shape[0]
    start = jnp.where(lax.axis_index("section") == 0, latents[0], in_flight[0])
    chunks = [swap(start, d) for d in range(group)]
    rows_modulation = jnp.transpose(modulation, (1, 0, 2))
    places = Places(w_qkv.shape[1], w_qkv.shape[3], w_expand.shape[2])
    qkv, expand, back, stale, later = load(
        places, jnp.transpose(w_qkv[0], (1, 0, 2)), w_expand[0], stale_kv[0], latents
    )
    weights = (w_expand[0], w_out[0], w_contract[0])
    chips = group // 2
    early = [swap(later, 2 * e) for e in range(chips)]
    result, fresh_all, section_out = None, None, None
    for tick in range(micro):
        held = (qkv, expand, back)
        kept, sent, fresh_all, *others = block(
            tick, micro, group, places, chunks, rows_modulation, qk_gain[0], stale, held, weights, result, section_out, fresh_all
        )
        if tick == 0:
            expand, back, inputs = others
        else:
            (section_out,) = others
        sums = add_pair(kept, swap(sent, 1), chips, early[1:] if tick == 0 else ())
        parts = [swap(sums[e], 2 * e) for e in range(chips)]
        if tick == micro - 1:
            section_out = finish_last(tick, parts, inputs, rows_modulation, section_out)
        else:
            (result,) = small(finish_kernel, "finish", [parts[0].shape], (*parts, inputs, rows_modulation))
            passed = [to_next_section(result, 2 * e) for e in range(chips)]
            (inputs,) = small(functools.partial(enter_kernel, tick), "enter", [inputs.shape], (*passed, *early))
            chunks = [inputs, swap(inputs, 1)]
    return (section_out[None], fresh_all[None])


def solution(mesh):
    placed = (
        P(None, "sp", None),
        P("section", "sp", None),
        P("section", None, None),
        P("section", None, None, "sp"),
        P("section", None, "sp"),
        P("section", None, None),
        P("section", "sp", None),
        P("section", "sp", None),
        P("section", None, None, "sp"),
    )
    return jax.shard_map(
        local,
        mesh=mesh,
        in_specs=placed,
        out_specs=(P("section", None, "sp", None), P("section", None, None, None, "sp")),
        check_vma=False,
    )
```
